256 devices in a mesh: branch: 2 (over core), group: 4 (over y), seq: 32 (over z, x).
Axes of the slice: x: 4, y: 4, z: 8, core: 2. Of those that a mesh axis runs over, the one named last changes fastest.
Arguments:
- qkv: bfloat16 [2, 16384, 3, 3072], P('branch', ('group', 'seq')), parts along dimension 1, may hold values from -18 to 18
- tiles: int32 [96, 32, 32], P('group'), parts along dimension 0, may hold values from 0 to 1, as said below
Outputs:
- guided: bfloat16 [16384, 3072], P(('group', 'seq'), 'branch'), parts along dimension 0
The draws below stay inside these ranges and needn't reach their ends.
There are 4 independent parts, one for each index of `group`. The reference program is written for one: setup_inputs(seed, part) draws one part's arguments, and reference() takes and returns one part's arrays. A program takes and returns all parts, laid end to end along the dimension named above; each array names one. Nothing has to cross between parts.
Inputs may be any that keep to these rules, and one draw needn't show every extreme that they name: Every head's mask holds its diagonal tiles.
All inputs are finite; a program needn't handle non-finite values.
Results may differ from the reference program's by a relative error of at most 0.0057.
Values may be sent and summed in bfloat16 or wider, within the bound.
A program may use at most 64 MiB of HBM per device.

```python
import math
import jax
import jax.numpy as jnp
from jax import lax

H = 24
DH = 128
FT = 4
S = 4096
NT = 32


def draw_qkv(key, part):
    key = jax.random.fold_in(key, 5)
    full_shape = (2, S, 3, H * DH)
    return jnp.clip(jax.random.normal(key, full_shape, jnp.float32), -6.0, 6.0).astype(jnp.bfloat16)


def draw_tiles(key, part):
    key = jax.random.fold_in(key, 11)
    key_one, key_two, key_three = jax.random.split(key, 3)
    head_kind = jax.random.randint(key_one, (H, 1, 1), 0, 2)
    frame_reach = jax.random.randint(key_two, (H, 1, 1), 1, 4)
    row_ids = jnp.arange(NT)[None, :, None]
    col_ids = jnp.arange(NT)[None, None, :]
    spatial = jnp.abs(row_ids // FT - col_ids // FT) < frame_reach
    temporal = row_ids % FT == col_ids % FT
    sprinkle = jax.random.randint(key_three, (H, NT, NT), 0, 8) == 0
    chosen = jnp.where(head_kind == 1, temporal, spatial)
    return (chosen | sprinkle).astype(jnp.int32)


def setup_inputs(seed: int = 0, part: int = 0) -> dict:
    arg_keys = jax.random.split(jax.random.key(seed), 3)
    part_keys = jax.random.split(jax.random.fold_in(arg_keys[2], part), 3)
    return {
        "qkv": draw_qkv(jax.random.fold_in(jax.random.fold_in(arg_keys[2], part), 71), part),
        "tiles": draw_tiles(jax.random.fold_in(jax.random.fold_in(arg_keys[2], part), 71), part),
    }


GUIDE = 5.0

def masked_block(query_rows, key_rows, value_rows, tile_rows, tile_len):
    scores = jnp.dot(query_rows, key_rows.T, preferred_element_type=jnp.float32) * (1.0 / math.sqrt(query_rows.shape[1]))
    allowed = jnp.repeat(jnp.repeat(tile_rows == 1, tile_len, axis=0), tile_len, axis=1)
    scores = jnp.where(allowed, scores, -1e+30)
    row_max = lax.optimization_barrier(jnp.max(scores, axis=1, keepdims=True))
    exponent = jnp.where(allowed, jnp.exp(scores - row_max), 0.0)
    row_total = lax.optimization_barrier(jnp.sum(exponent, axis=1, keepdims=True))
    weights = exponent.astype(jnp.bfloat16)
    mixed_rows = jnp.dot(weights, value_rows, preferred_element_type=jnp.float32)
    return (mixed_rows / row_total).astype(jnp.bfloat16)

def attend_rows(query_rows, key_rows, value_rows, tile_rows, tile_len):
    row_count = query_rows.shape[0]
    block_len = min(512, row_count)

    def single(position):
        query_block = lax.dynamic_slice_in_dim(query_rows, position * block_len, block_len, 0)
        tile_block = lax.dynamic_slice_in_dim(tile_rows, position * (block_len // tile_len), block_len // tile_len, 0)
        return masked_block(query_block, key_rows, value_rows, tile_block, tile_len)
    result = lax.map(single, jnp.arange(row_count // block_len, dtype=jnp.int32))
    return result.reshape(row_count, -1)

def reference(qkv, tiles):
    seq_len = qkv.shape[1]
    head_count = tiles.shape[0]
    head_size = qkv.shape[3] // head_count
    tile_len = seq_len // tiles.shape[1]
    outputs = []
    for branch_id in range(2):
        stacked = qkv[branch_id].reshape(seq_len, 3, head_count, head_size).transpose(2, 1, 0, 3)

        def per_head(head_pair):
            head_rows, head_tiles = head_pair
            return attend_rows(head_rows[0], head_rows[1], head_rows[2], head_tiles, tile_len)
        attended = lax.map(per_head, (stacked, tiles))
        outputs.append(attended.transpose(1, 0, 2).reshape(seq_len, head_count * head_size))
    cond_out = outputs[0].astype(jnp.float32)
    uncond_out = outputs[1].astype(jnp.float32)
    return (uncond_out + GUIDE * (cond_out - uncond_out)).astype(jnp.bfloat16)
```

```python
import functools
import math

import jax
import jax.numpy as jnp
from jax import lax
from jax.experimental import pallas as pl
from jax.experimental.pallas import tpu as pltpu
from jax.sharding import PartitionSpec as P

MESH = pl.DeviceIdType.MESH
GUIDE = 5.0
MASKED = -1e30

PLANES, WIDTH = 8, 4
CHIPS = PLANES * WIDTH
HEADS_IN_PLANE = 3
TOK = 128
DH = 128
SEQ = CHIPS * TOK
PAIR = 2
BQ = PAIR * TOK
BLOCKS = CHIPS // PAIR
KC = 1024
CHUNKS = SEQ // KC
ONES_ROWS = 16


def offset(n):
    distance = lax.rem(n, 4)
    rest = n // 4
    dx = rest // 2
    backward = lax.rem(rest, 2)
    dz = jnp.where(backward == 0, distance, jnp.where(distance == 0, 4, PLANES - distance))
    return dz, dx


def to_partner(z, x, n):
    dz, dx = offset(n)
    return lax.rem(z + dz, PLANES), lax.rem(x + dx, WIDTH)


def from_partner(z, x, n):
    dz, dx = offset(n)
    return lax.rem(z - dz + PLANES, PLANES), lax.rem(x - dx + WIDTH, WIDTH)


def place_of(z, x):
    return lax.rem(x - lax.rem(z, WIDTH) - 1 + 2 * WIDTH, WIDTH)


def rows_of(index):
    return pl.ds(pl.multiple_of(index * TOK, TOK), TOK)


def kernel(
    send_ref, tiles_ref, out_ref,
    k_buf, v_buf, q_buf, key_hot, v_t, bias, s_a, s_b, own_o, partner_o, mixed,
    kv_send, kv_recv, q_send, q_recv, pair_send, pair_recv, o_send, o_recv, local_sem,
):
    seq = lax.axis_index("seq")
    branch = lax.axis_index("branch")
    z, x = seq // WIDTH, lax.rem(seq, WIDTH)
    place = place_of(z, x)
    owner = place < HEADS_IN_PLANE
    head = z * HEADS_IN_PLANE + jnp.minimum(place, HEADS_IN_PLANE - 1)
    heads_of_half = out_ref.shape[1] // DH
    my_half = head // heads_of_half
    combines = my_half == branch

    barrier = pltpu.get_barrier_semaphore()

    def greet(n, carry):
        pz, px = to_partner(z, x, n)
        pl.semaphore_signal(barrier, inc=1, device_id={"seq": pz * WIDTH + px}, device_id_type=MESH)
        return carry

    lax.fori_loop(1, CHIPS, greet, 0)
    pl.semaphore_signal(barrier, inc=1, device_id={"branch": 1 - branch}, device_id_type=MESH)
    pl.semaphore_wait(barrier, CHIPS)

    def key_copy(n, pz, px, row):
        chosen = pz * HEADS_IN_PLANE + jnp.minimum(place_of(pz, px), HEADS_IN_PLANE - 1)
        return pltpu.make_async_remote_copy(
            src_ref=send_ref.at[chosen, 0], dst_ref=k_buf.at[rows_of(row)],
            send_sem=kv_send.at[0, n], recv_sem=kv_recv.at[0, n],
            device_id={"seq": pz * WIDTH + px}, device_id_type=MESH)

    def value_copy(n, pz, px, row):
        chosen = pz * HEADS_IN_PLANE + jnp.minimum(place_of(pz, px), HEADS_IN_PLANE - 1)
        return pltpu.make_async_remote_copy(
            src_ref=send_ref.at[chosen, 1], dst_ref=v_buf.at[rows_of(row)],
            send_sem=kv_send.at[1, n], recv_sem=kv_recv.at[1, n],
            device_id={"seq": pz * WIDTH + px}, device_id_type=MESH)

    def query_copy(n, pz, px):
        chosen = pz * HEADS_IN_PLANE + jnp.minimum(place_of(pz, px), HEADS_IN_PLANE - 1)
        return pltpu.make_async_remote_copy(
            src_ref=send_ref.at[chosen, 2], dst_ref=q_buf.at[rows_of(n)],
            send_sem=q_send.at[n], recv_sem=q_recv.at[n],
            device_id={"seq": pz * WIDTH + px}, device_id_type=MESH)

    def own_copies():
        return (
            pltpu.make_async_copy(send_ref.at[head, 0], k_buf.at[rows_of(seq)], local_sem.at[0]),
            pltpu.make_async_copy(send_ref.at[head, 1], v_buf.at[rows_of(seq)], local_sem.at[1]),
            pltpu.make_async_copy(send_ref.at[head, 2], q_buf.at[rows_of(0)], local_sem.at[2]),
        )

    def send_kv(n, carry):
        pz, px = to_partner(z, x, n)

        @pl.when(place_of(pz, px) < HEADS_IN_PLANE)
        def _():
            key_copy(n, pz, px, seq).start()
            value_copy(n, pz, px, seq).start()
        return carry

    lax.fori_loop(1, CHIPS, send_kv, 0)

    @pl.when(owner)
    def _():
        for copy in own_copies():
            copy.start()

    lane = lax.broadcasted_iota(jnp.int32, (TOK, DH), 1)

    def fill_hot(t, carry):
        key_hot[rows_of(t), :] = jnp.where(lane == t, 1.0, 0.0).astype(jnp.bfloat16)
        return carry

    lax.fori_loop(0, CHIPS, fill_hot, 0)
    v_t[DH:DH + ONES_ROWS, :] = jnp.ones((ONES_ROWS, SEQ), jnp.bfloat16)
    bias[...] = jnp.zeros_like(bias)
    bias[:, 0:CHIPS] = jnp.where(tiles_ref[head] == 1, 0.0, MASKED)

    def turn_value(row):
        v_t[0:DH, rows_of(row)] = v_buf[rows_of(row), :].T

    def wait_kv_sent(n, carry):
        pz, px = to_partner(z, x, n)

        @pl.when(place_of(pz, px) < HEADS_IN_PLANE)
        def _():
            key_copy(n, pz, px, seq).wait_send()
            value_copy(n, pz, px, seq).wait_send()
        return carry

    def send_q(n, carry):
        pz, px = to_partner(z, x, n)

        @pl.when(place_of(pz, px) < HEADS_IN_PLANE)
        def _():
            query_copy(n, pz, px).start()
        return carry

    def wait_q_sent(n, carry):
        pz, px = to_partner(z, x, n)

        @pl.when(place_of(pz, px) < HEADS_IN_PLANE)
        def _():
            query_copy(n, pz, px).wait_send()
        return carry

    lax.fori_loop(1, CHIPS, wait_kv_sent, 0)
    lax.fori_loop(1, CHIPS, send_q, 0)

    def pair_copy(block):
        return pltpu.make_async_remote_copy(
            src_ref=own_o.at[block], dst_ref=partner_o.at[block],
            send_sem=pair_send.at[block], recv_sem=pair_recv.at[block],
            device_id={"branch": 1 - branch}, device_id_type=MESH)

    out_columns = pl.ds(pl.multiple_of(lax.rem(head, heads_of_half) * DH, DH), DH)

    def result_copy(n, block, part):
        pz, px = from_partner(z, x, n)
        return pltpu.make_async_remote_copy(
            src_ref=mixed.at[block, pl.ds(part * TOK, TOK)], dst_ref=out_ref.at[:, out_columns],
            send_sem=o_send.at[n], recv_sem=o_recv.at[lax.rem(head, heads_of_half)],
            device_id={"seq": pz * WIDTH + px}, device_id_type=MESH)

    def own_result_copy():
        return pltpu.make_async_copy(
            mixed.at[0, pl.ds(0, TOK)], out_ref.at[:, out_columns], local_sem.at[3])

    def combine(block):
        pair_copy(block).wait_recv()
        mine = own_o[block].astype(jnp.float32)
        other = partner_o[block].astype(jnp.float32)
        cond = jnp.where(branch == 0, mine, other)
        uncond = jnp.where(branch == 0, other, mine)
        mixed[block] = (uncond + GUIDE * (cond - uncond)).astype(jnp.bfloat16)
        for part in range(PAIR):
            n = block * PAIR + part

            @pl.when(n == 0)
            def _():
                own_result_copy().start()

            @pl.when(n != 0)
            def _():
                result_copy(n, block, part).start()

    def wait_query(n):
        pz, px = from_partner(z, x, n)
        pltpu.make_async_remote_copy(
            src_ref=send_ref.at[0, 2], dst_ref=q_buf.at[rows_of(n)],
            send_sem=q_send.at[n], recv_sem=q_recv.at[n],
            device_id={"seq": pz * WIDTH + px}, device_id_type=MESH).wait_recv()

    def extended_query(block):
        parts = []
        for part in range(PAIR):
            n = block * PAIR + part
            pz, px = from_partner(z, x, n)
            row = bias[pl.ds(pz * WIDTH + px, 1), :]
            parts.append(jnp.concatenate(
                [q_buf[rows_of(n), :], jnp.broadcast_to(row, (TOK, DH)).astype(jnp.bfloat16)], axis=1))
        return jnp.concatenate(parts, axis=0)

    scale = math.log2(math.e) / math.sqrt(DH)

    def score(query, s_ref, chunk, top):
        keys = jnp.concatenate(
            [k_buf[chunk * KC:(chunk + 1) * KC, :], key_hot[chunk * KC:(chunk + 1) * KC, :]], axis=1)
        s = lax.dot_general(keys, query, (((1,), (1,)), ((), ())), preferred_element_type=jnp.float32)
        s_ref[chunk * KC:(chunk + 1) * KC, :] = s
        return jnp.maximum(top, jnp.max(s.reshape(KC // 8, 8, BQ), axis=0))

    def weigh(s_ref, top, chunk, total):
        s = s_ref[chunk * KC:(chunk + 1) * KC, :].reshape(KC // 8, 8, BQ)
        weights = jnp.exp2(s * scale - top[None]).reshape(KC, BQ).astype(jnp.bfloat16)
        return total + jnp.dot(
            v_t[:, chunk * KC:(chunk + 1) * KC], weights, preferred_element_type=jnp.float32)

    lowest = jnp.full((8, BQ), -3e38, jnp.float32)

    def settle(top):
        return jnp.broadcast_to(jnp.max(top, axis=0, keepdims=True) * scale, (8, BQ))

    def finish(block, total):
        inverse = 1.0 / total[DH:DH + 8, :]
        o = (total[:DH].reshape(DH // 8, 8, BQ) * inverse[None]).reshape(DH, BQ)
        own_o[block] = o.T.astype(jnp.bfloat16)

        @pl.when(jnp.logical_not(combines))
        def _():
            pair_copy(block).start()

    def half(block, following, top, s_now, s_next):
        @pl.when(following < BLOCKS)
        def _():
            for part in range(PAIR):
                wait_query(following * PAIR + part)

        query = extended_query(jnp.minimum(following, BLOCKS - 1))
        new_top = lowest
        total = jnp.zeros((DH + ONES_ROWS, BQ), jnp.float32)
        for chunk in range(CHUNKS):
            new_top = score(query, s_next, chunk, new_top)
            total = weigh(s_now, top, chunk, total)
        finish(block, total)

        @pl.when(jnp.logical_and(combines, block > 0))
        def _():
            combine(block - 1)
        return settle(new_top)

    @pl.when(owner)
    def _():
        for copy in own_copies():
            copy.wait()
        turn_value(seq)

        def take_kv(n, carry):
            pz, px = from_partner(z, x, n)
            row = pz * WIDTH + px
            key_copy(n, pz, px, row).wait_recv()
            value_copy(n, pz, px, row).wait_recv()
            turn_value(row)
            return carry

        lax.fori_loop(1, CHIPS, take_kv, 0)
        wait_query(1)
        query = extended_query(0)
        top = lowest
        for chunk in range(CHUNKS):
            top = score(query, s_a, chunk, top)
        top = settle(top)

        def two_blocks(step, top):
            top = half(2 * step, 2 * step + 1, top, s_a, s_b)
            return half(2 * step + 1, 2 * step + 2, top, s_b, s_a)

        lax.fori_loop(0, BLOCKS // 2, two_blocks, top)

        @pl.when(combines)
        def _():
            combine(BLOCKS - 1)
            own_result_copy().wait()

            def wait_result_sent(n, carry):
                result_copy(n, n // PAIR, lax.rem(n, PAIR)).wait_send()
                return carry

            lax.fori_loop(1, CHIPS, wait_result_sent, 0)

        @pl.when(jnp.logical_not(combines))
        def _():
            def wait_pair_sent(block, carry):
                pair_copy(block).wait_send()
                return carry

            lax.fori_loop(0, BLOCKS, wait_pair_sent, 0)

    lax.fori_loop(1, CHIPS, wait_q_sent, 0)

    def wait_result(column, carry):
        whole = branch * heads_of_half + column
        pz = whole // HEADS_IN_PLANE
        px = lax.rem(lax.rem(pz, WIDTH) + 1 + lax.rem(whole, HEADS_IN_PLANE), WIDTH)
        where = pl.ds(pl.multiple_of(column * DH, DH), DH)

        @pl.when(pz * WIDTH + px != seq)
        def _():
            pltpu.make_async_remote_copy(
                src_ref=mixed.at[0, pl.ds(0, TOK)], dst_ref=out_ref.at[:, where],
                send_sem=o_send.at[0], recv_sem=o_recv.at[column],
                device_id={"seq": pz * WIDTH + px}, device_id_type=MESH).wait_recv()
        return carry

    lax.fori_loop(0, heads_of_half, wait_result, 0)


def shards(qkv, tiles):
    tok_rows, width = qkv.shape[1], qkv.shape[3]
    head_count = tiles.shape[0]
    rows = qkv[0].reshape(tok_rows, 3, head_count, DH)
    outgoing = jnp.stack([rows[:, 1], rows[:, 2], rows[:, 0]]).transpose(2, 0, 1, 3)
    bf16, f32 = jnp.bfloat16, jnp.float32
    dma = pltpu.SemaphoreType.DMA
    return pl.pallas_call(
        kernel,
        out_shape=jax.ShapeDtypeStruct((tok_rows, width // 2), bf16),
        in_specs=[pl.BlockSpec(memory_space=pl.ANY), pl.BlockSpec(memory_space=pltpu.VMEM)],
        out_specs=pl.BlockSpec(memory_space=pltpu.VMEM),
        scratch_shapes=[
            pltpu.VMEM((SEQ, DH), bf16),
            pltpu.VMEM((SEQ, DH), bf16),
            pltpu.VMEM((SEQ, DH), bf16),
            pltpu.VMEM((SEQ, DH), bf16),
            pltpu.VMEM((DH + ONES_ROWS, SEQ), bf16),
            pltpu.VMEM((CHIPS, DH), f32),
            pltpu.VMEM((SEQ, BQ), f32),
            pltpu.VMEM((SEQ, BQ), f32),
            pltpu.VMEM((BLOCKS, BQ, DH), bf16),
            pltpu.VMEM((BLOCKS, BQ, DH), bf16),
            pltpu.VMEM((BLOCKS, BQ, DH), bf16),
            dma((2, CHIPS)), dma((2, CHIPS)),
            dma((CHIPS,)), dma((CHIPS,)),
            dma((BLOCKS,)), dma((BLOCKS,)),
            dma((CHIPS,)), dma((head_count // 2,)),
            dma((4,)),
        ],
        compiler_params=pltpu.CompilerParams(
            collective_id=0, has_side_effects=True, vmem_limit_bytes=48 * 2**20),
        cost_estimate=pl.CostEstimate(
            flops=4 * SEQ * SEQ * DH, bytes_accessed=4 * SEQ * DH * 2, transcendentals=SEQ * SEQ),
    )(outgoing, tiles)


def solution(mesh):
    in_specs = (P("branch", ("group", "seq"), None, None), P("group", None, None))
    out_specs = P(("group", "seq"), "branch")
    return jax.shard_map(shards, mesh=mesh, in_specs=in_specs, out_specs=out_specs, check_vma=False)
```

```python
import functools
import math

import jax
import jax.numpy as jnp
from jax import lax
from jax.experimental import pallas as pl
from jax.experimental.pallas import tpu as pltpu
from jax.sharding import PartitionSpec as P

MESH = pl.DeviceIdType.MESH
GUIDE = 5.0
GATE = 1
MASKED = -1e30

PLANES, WIDTH = 8, 4
CHIPS = PLANES * WIDTH
HEADS_IN_PLANE = 3
TOK = 128
DH = 128
SEQ = CHIPS * TOK
PAIR = 2
BQ = PAIR * TOK
BLOCKS = CHIPS // PAIR
KC = 1024
CHUNKS = SEQ // KC


def offset(n):
    turn = lax.rem(n, PLANES)
    distance = turn // 2
    backward = lax.rem(turn, 2)
    dx = lax.rem(n // PLANES + turn, WIDTH)
    dz = jnp.where(backward == 0, distance, jnp.where(distance == 0, 4, PLANES - distance))
    return dz, dx


def to_partner(z, x, n):
    dz, dx = offset(n)
    return lax.rem(z + dz, PLANES), lax.rem(x + dx, WIDTH)


def from_partner(z, x, n):
    dz, dx = offset(n)
    return lax.rem(z - dz + PLANES, PLANES), lax.rem(x - dx + WIDTH, WIDTH)


def owned_head(z, x):
    return z * HEADS_IN_PLANE + jnp.minimum(x, HEADS_IN_PLANE - 1)


def rows_of(index):
    return pl.ds(pl.multiple_of(index * TOK, TOK), TOK)


def kernel(
    send_ref, tiles_ref, out_ref,
    k_buf, v_buf, q_buf, key_hot, v_t, tile_buf, bias, s_a, s_b, own_o, partner_o, mixed,
    kv_send, kv_recv, q_send, q_recv, pair_send, pair_recv, o_send, o_recv, local_sem,
):
    seq = lax.axis_index("seq")
    branch = lax.axis_index("branch")
    z, x = seq // WIDTH, lax.rem(seq, WIDTH)
    owner = x < HEADS_IN_PLANE
    head = owned_head(z, x)
    heads_of_half = out_ref.shape[1] // DH
    my_half = head // heads_of_half
    combines = my_half == branch

    tiles_copy = pltpu.make_async_copy(tiles_ref.at[head], tile_buf, local_sem.at[4])
    tiles_copy.start()
    barrier = pltpu.get_barrier_semaphore()

    def greet(n, carry):
        pz, px = to_partner(z, x, n)
        pl.semaphore_signal(barrier, inc=1, device_id={"seq": pz * WIDTH + px}, device_id_type=MESH)
        return carry

    lax.fori_loop(1, CHIPS, greet, 0)
    pl.semaphore_signal(barrier, inc=1, device_id={"branch": 1 - branch}, device_id_type=MESH)
    pl.semaphore_wait(barrier, CHIPS)

    def block_of(which, part):
        return send_ref.at[part, :, pl.ds(pl.multiple_of(which * DH, DH), DH)]

    def key_copy(n, pz, px, row):
        chosen = owned_head(pz, px)
        return pltpu.make_async_remote_copy(
            src_ref=block_of(chosen, 1), dst_ref=k_buf.at[rows_of(row)],
            send_sem=kv_send.at[0, n], recv_sem=kv_recv.at[0, n],
            device_id={"seq": pz * WIDTH + px}, device_id_type=MESH)

    def value_copy(n, pz, px, row):
        chosen = owned_head(pz, px)
        return pltpu.make_async_remote_copy(
            src_ref=block_of(chosen, 2), dst_ref=v_buf.at[rows_of(row)],
            send_sem=kv_send.at[1, n], recv_sem=kv_recv.at[1, n],
            device_id={"seq": pz * WIDTH + px}, device_id_type=MESH)

    def query_copy(n, pz, px):
        chosen = owned_head(pz, px)
        return pltpu.make_async_remote_copy(
            src_ref=block_of(chosen, 0), dst_ref=q_buf.at[rows_of(n)],
            send_sem=q_send.at[n], recv_sem=q_recv.at[n],
            device_id={"seq": pz * WIDTH + px}, device_id_type=MESH)

    def own_copies():
        return (
            pltpu.make_async_copy(block_of(head, 1), k_buf.at[rows_of(seq)], local_sem.at[0]),
            pltpu.make_async_copy(block_of(head, 2), v_buf.at[rows_of(seq)], local_sem.at[1]),
            pltpu.make_async_copy(block_of(head, 0), q_buf.at[rows_of(0)], local_sem.at[2]),
        )

    def send_kv(n, carry):
        pz, px = to_partner(z, x, n)

        @pl.when(px < HEADS_IN_PLANE)
        def _():
            key_copy(n, pz, px, seq).start()
            value_copy(n, pz, px, seq).start()
        return carry

    lax.fori_loop(1, CHIPS, send_kv, 0)

    @pl.when(owner)
    def _():
        for copy in own_copies():
            copy.start()

    lane = lax.broadcasted_iota(jnp.int32, (TOK, DH), 1)

    def fill_hot(t, carry):
        key_hot[rows_of(t), :] = jnp.where(lane == t, 1.0, 0.0).astype(jnp.bfloat16)
        return carry

    lax.fori_loop(0, CHIPS, fill_hot, 0)
    bias[...] = jnp.zeros_like(bias)
    tiles_copy.wait()
    bias[:, 0:CHIPS] = jnp.where(tile_buf[...] == 1, 0.0, MASKED)

    def turn_value(row):
        v_t[:, rows_of(row)] = v_buf[rows_of(row), :].T

    def wait_kv_sent(n, carry):
        pz, px = to_partner(z, x, n)

        @pl.when(px < HEADS_IN_PLANE)
        def _():
            key_copy(n, pz, px, seq).wait_send()
            value_copy(n, pz, px, seq).wait_send()
        return carry

    def send_q(n, carry):
        pz, px = to_partner(z, x, n)

        @pl.when(px < HEADS_IN_PLANE)
        def _():
            query_copy(n, pz, px).start()
        return carry

    def wait_q_sent(n, carry):
        pz, px = to_partner(z, x, n)

        @pl.when(px < HEADS_IN_PLANE)
        def _():
            query_copy(n, pz, px).wait_send()
        return carry

    lax.fori_loop(1, GATE, wait_kv_sent, 0)
    lax.fori_loop(1, CHIPS, send_q, 0)

    def pair_copy(block):
        return pltpu.make_async_remote_copy(
            src_ref=own_o.at[block], dst_ref=partner_o.at[block],
            send_sem=pair_send.at[block], recv_sem=pair_recv.at[block],
            device_id={"branch": 1 - branch}, device_id_type=MESH)

    out_columns = pl.ds(pl.multiple_of(lax.rem(head, heads_of_half) * DH, DH), DH)

    def result_copy(n, block, part):
        pz, px = from_partner(z, x, n)
        return pltpu.make_async_remote_copy(
            src_ref=mixed.at[block, pl.ds(part * TOK, TOK)], dst_ref=out_ref.at[:, out_columns],
            send_sem=o_send.at[n], recv_sem=o_recv.at[lax.rem(head, heads_of_half)],
            device_id={"seq": pz * WIDTH + px}, device_id_type=MESH)

    def own_result_copy():
        return pltpu.make_async_copy(
            mixed.at[0, pl.ds(0, TOK)], out_ref.at[:, out_columns], local_sem.at[3])

    def combine(block):
        pair_copy(block).wait_recv()
        mine = own_o[block].astype(jnp.float32)
        other = partner_o[block].astype(jnp.float32)
        cond = jnp.where(branch == 0, mine, other)
        uncond = jnp.where(branch == 0, other, mine)
        mixed[block] = (uncond + GUIDE * (cond - uncond)).astype(jnp.bfloat16)
        for part in range(PAIR):
            n = block * PAIR + part

            @pl.when(n == 0)
            def _():
                own_result_copy().start()

            @pl.when(n != 0)
            def _():
                result_copy(n, block, part).start()

    def wait_query(n):
        pz, px = from_partner(z, x, n)
        pltpu.make_async_remote_copy(
            src_ref=block_of(0, 0), dst_ref=q_buf.at[rows_of(n)],
            send_sem=q_send.at[n], recv_sem=q_recv.at[n],
            device_id={"seq": pz * WIDTH + px}, device_id_type=MESH).wait_recv()

    def extended_query(block):
        parts = []
        for part in range(PAIR):
            n = block * PAIR + part
            pz, px = from_partner(z, x, n)
            row = bias[pl.ds(pz * WIDTH + px, 1), :]
            parts.append(jnp.concatenate(
                [q_buf[rows_of(n), :], jnp.broadcast_to(row, (TOK, DH)).astype(jnp.bfloat16)], axis=1))
        return jnp.concatenate(parts, axis=0)

    scale = math.log2(math.e) / math.sqrt(DH)

    def score(query, s_ref, chunk, top):
        keys = jnp.concatenate(
            [k_buf[chunk * KC:(chunk + 1) * KC, :], key_hot[chunk * KC:(chunk + 1) * KC, :]], axis=1)
        s = lax.dot_general(keys, query, (((1,), (1,)), ((), ())), preferred_element_type=jnp.float32)
        s_ref[chunk * KC:(chunk + 1) * KC, :] = s
        return jnp.maximum(top, jnp.max(s.reshape(KC // 8, 8, BQ), axis=0))

    def weigh(s_ref, top, chunk, total, row_total):
        s = s_ref[chunk * KC:(chunk + 1) * KC, :].reshape(KC // 8, 8, BQ)
        exponent = jnp.exp2(s * scale - top[None])
        weights = exponent.reshape(KC, BQ).astype(jnp.bfloat16)
        total = total + jnp.dot(
            v_t[:, chunk * KC:(chunk + 1) * KC], weights, preferred_element_type=jnp.float32)
        return total, row_total + jnp.sum(exponent, axis=0)

    lowest = jnp.full((8, BQ), -3e38, jnp.float32)

    def settle(top):
        return jnp.broadcast_to(jnp.max(top, axis=0, keepdims=True) * scale, (8, BQ))

    def finish(block, total, row_total):
        inverse = jnp.broadcast_to(1.0 / jnp.sum(row_total, axis=0, keepdims=True), (8, BQ))
        o = (total.reshape(DH // 8, 8, BQ) * inverse[None]).reshape(DH, BQ)
        own_o[block] = o.T.astype(jnp.bfloat16)

        @pl.when(jnp.logical_not(combines))
        def _():
            pair_copy(block).start()

    def half(block, following, top, s_now, s_next):
        if following is not None:
            for part in range(PAIR):
                wait_query(following * PAIR + part)
            query = extended_query(following)
        new_top = lowest
        total = jnp.zeros((DH, BQ), jnp.float32)
        row_total = jnp.zeros((8, BQ), jnp.float32)
        for chunk in range(CHUNKS):
            if following is not None:
                new_top = score(query, s_next, chunk, new_top)
            total, row_total = weigh(s_now, top, chunk, total, row_total)
        finish(block, total, row_total)

        @pl.when(jnp.logical_and(combines, block > 0))
        def _():
            combine(block - 1)
        return settle(new_top)

    @pl.when(owner)
    def _():
        for copy in own_copies():
            copy.wait()
        turn_value(seq)

        def take_kv(n, carry):
            pz, px = from_partner(z, x, n)
            row = pz * WIDTH + px
            key_copy(n, pz, px, row).wait_recv()
            value_copy(n, pz, px, row).wait_recv()
            turn_value(row)
            return carry

        lax.fori_loop(1, CHIPS, take_kv, 0)
        wait_query(1)
        query = extended_query(0)
        top = lowest
        for chunk in range(CHUNKS):
            top = score(query, s_a, chunk, top)
        top = settle(top)

        def two_blocks(step, top):
            top = half(2 * step, 2 * step + 1, top, s_a, s_b)
            return half(2 * step + 1, 2 * step + 2, top, s_b, s_a)

        top = lax.fori_loop(0, BLOCKS // 2 - 1, two_blocks, top)
        top = half(BLOCKS - 2, BLOCKS - 1, top, s_a, s_b)
        half(BLOCKS - 1, None, top, s_b, s_a)

        @pl.when(combines)
        def _():
            combine(BLOCKS - 1)
            own_result_copy().wait()

            def wait_result_sent(n, carry):
                result_copy(n, n // PAIR, lax.rem(n, PAIR)).wait_send()
                return carry

            lax.fori_loop(1, CHIPS, wait_result_sent, 0)

        @pl.when(jnp.logical_not(combines))
        def _():
            def wait_pair_sent(block, carry):
                pair_copy(block).wait_send()
                return carry

            lax.fori_loop(0, BLOCKS, wait_pair_sent, 0)

    lax.fori_loop(GATE, CHIPS, wait_kv_sent, 0)
    lax.fori_loop(1, CHIPS, wait_q_sent, 0)

    def wait_result(column, carry):
        whole = branch * heads_of_half + column
        pz = whole // HEADS_IN_PLANE
        px = lax.rem(whole, HEADS_IN_PLANE)
        where = pl.ds(pl.multiple_of(column * DH, DH), DH)

        @pl.when(pz * WIDTH + px != seq)
        def _():
            pltpu.make_async_remote_copy(
                src_ref=mixed.at[0, pl.ds(0, TOK)], dst_ref=out_ref.at[:, where],
                send_sem=o_send.at[0], recv_sem=o_recv.at[column],
                device_id={"seq": pz * WIDTH + px}, device_id_type=MESH).wait_recv()
        return carry

    lax.fori_loop(0, heads_of_half, wait_result, 0)


def shards(qkv, tiles):
    tok_rows, width = qkv.shape[1], qkv.shape[3]
    head_count = tiles.shape[0]
    outgoing = qkv[0].transpose(1, 0, 2)
    bf16, f32 = jnp.bfloat16, jnp.float32
    dma = pltpu.SemaphoreType.DMA
    return pl.pallas_call(
        kernel,
        out_shape=pltpu.VMEM((tok_rows, width // 2), bf16),
        in_specs=[pl.BlockSpec(memory_space=pl.ANY), pl.BlockSpec(memory_space=pl.ANY)],
        out_specs=pl.BlockSpec(memory_space=pltpu.VMEM),
        scratch_shapes=[
            pltpu.VMEM((SEQ, DH), bf16),
            pltpu.VMEM((SEQ, DH), bf16),
            pltpu.VMEM((SEQ, DH), bf16),
            pltpu.VMEM((SEQ, DH), bf16),
            pltpu.VMEM((DH, SEQ), bf16),
            pltpu.VMEM((CHIPS, CHIPS), jnp.int32),
            pltpu.VMEM((CHIPS, DH), f32),
            pltpu.VMEM((SEQ, BQ), f32),
            pltpu.VMEM((SEQ, BQ), f32),
            pltpu.VMEM((BLOCKS, BQ, DH), bf16),
            pltpu.VMEM((BLOCKS, BQ, DH), bf16),
            pltpu.VMEM((BLOCKS, BQ, DH), bf16),
            dma((2, CHIPS)), dma((2, CHIPS)),
            dma((CHIPS,)), dma((CHIPS,)),
            dma((BLOCKS,)), dma((BLOCKS,)),
            dma((CHIPS,)), dma((head_count // 2,)),
            dma((5,)),
        ],
        compiler_params=pltpu.CompilerParams(
            collective_id=0, has_side_effects=True, vmem_limit_bytes=60 * 2**20),
        cost_estimate=pl.CostEstimate(
            flops=4 * SEQ * SEQ * DH, bytes_accessed=4 * SEQ * DH * 2, transcendentals=SEQ * SEQ),
    )(outgoing, tiles)


def solution(mesh):
    in_specs = (P("branch", ("group", "seq"), None, None), P("group", None, None))
    out_specs = P(("group", "seq"), "branch")
    return jax.shard_map(shards, mesh=mesh, in_specs=in_specs, out_specs=out_specs, check_vma=False)
```

```python
import functools
import math

import jax
import jax.numpy as jnp
from jax import lax
from jax.experimental import pallas as pl
from jax.experimental.pallas import tpu as pltpu
from jax.sharding import PartitionSpec as P

MESH = pl.DeviceIdType.MESH
GUIDE = 5.0
MASKED = -1e30

PLANES, WIDTH = 8, 4
CHIPS = PLANES * WIDTH
HEADS_IN_PLANE = 3
TOK = 128
DH = 128
SEQ = CHIPS * TOK
PAIR = 2
BQ = PAIR * TOK
BLOCKS = CHIPS // PAIR
KC = 1024
CHUNKS = SEQ // KC


def offset(n):
    turn = lax.rem(n, PLANES)
    distance = turn // 2
    backward = lax.rem(turn, 2)
    dx = lax.rem(n // PLANES + turn, WIDTH)
    dz = jnp.where(backward == 0, distance, jnp.where(distance == 0, 4, PLANES - distance))
    return dz, dx


def to_partner(z, x, n):
    dz, dx = offset(n)
    return lax.rem(z + dz, PLANES), lax.rem(x + dx, WIDTH)


def from_partner(z, x, n):
    dz, dx = offset(n)
    return lax.rem(z - dz + PLANES, PLANES), lax.rem(x - dx + WIDTH, WIDTH)


def owned_head(z, x):
    return z * HEADS_IN_PLANE + jnp.minimum(x, HEADS_IN_PLANE - 1)


def rows_of(index):
    return pl.ds(pl.multiple_of(index * TOK, TOK), TOK)


def kernel(
    send_ref, tiles_ref, out_ref,
    k_buf, v_buf, q_buf, key_hot, v_t, tile_buf, bias, s_a, s_b, own_o, partner_o, mixed,
    kv_send, kv_recv, q_send, q_recv, pair_send, pair_recv, o_send, o_recv, local_sem,
):
    seq = lax.axis_index("seq")
    branch = lax.axis_index("branch")
    z, x = seq // WIDTH, lax.rem(seq, WIDTH)
    owner = x < HEADS_IN_PLANE
    head = owned_head(z, x)
    heads_of_half = out_ref.shape[1] // DH
    my_half = head // heads_of_half
    combines = my_half == branch

    tiles_copy = pltpu.make_async_copy(tiles_ref.at[head], tile_buf, local_sem.at[4])
    tiles_copy.start()
    barrier = pltpu.get_barrier_semaphore()

    def greet(n, carry):
        pz, px = to_partner(z, x, n)
        pl.semaphore_signal(barrier, inc=1, device_id={"seq": pz * WIDTH + px}, device_id_type=MESH)
        return carry

    lax.fori_loop(1, CHIPS, greet, 0)
    pl.semaphore_signal(barrier, inc=1, device_id={"branch": 1 - branch}, device_id_type=MESH)
    pl.semaphore_wait(barrier, CHIPS)

    def block_of(which, part):
        return send_ref.at[part, :, pl.ds(pl.multiple_of(which * DH, DH), DH)]

    def key_copy(pz, px):
        chosen = owned_head(pz, px)
        return pltpu.make_async_remote_copy(
            src_ref=block_of(chosen, 1), dst_ref=k_buf.at[rows_of(seq)],
            send_sem=kv_send.at[0], recv_sem=kv_recv.at[0],
            device_id={"seq": pz * WIDTH + px}, device_id_type=MESH)

    def value_copy(pz, px):
        chosen = owned_head(pz, px)
        return pltpu.make_async_remote_copy(
            src_ref=block_of(chosen, 2), dst_ref=v_buf.at[rows_of(seq)],
            send_sem=kv_send.at[1], recv_sem=kv_recv.at[1],
            device_id={"seq": pz * WIDTH + px}, device_id_type=MESH)

    def query_copy(n, pz, px):
        chosen = owned_head(pz, px)
        return pltpu.make_async_remote_copy(
            src_ref=block_of(chosen, 0), dst_ref=q_buf.at[rows_of(n)],
            send_sem=q_send.at[0], recv_sem=q_recv.at[n // PAIR],
            device_id={"seq": pz * WIDTH + px}, device_id_type=MESH)

    def own_copies():
        return (
            pltpu.make_async_copy(block_of(head, 1), k_buf.at[rows_of(seq)], local_sem.at[0]),
            pltpu.make_async_copy(block_of(head, 2), v_buf.at[rows_of(seq)], local_sem.at[1]),
            pltpu.make_async_copy(block_of(head, 0), q_buf.at[rows_of(0)], local_sem.at[2]),
        )

    def send_kv(n, carry):
        pz, px = to_partner(z, x, n)

        @pl.when(px < HEADS_IN_PLANE)
        def _():
            key_copy(pz, px).start()
            value_copy(pz, px).start()
        return carry

    lax.fori_loop(1, CHIPS, send_kv, 0)

    @pl.when(owner)
    def _():
        for copy in own_copies():
            copy.start()

    lane = lax.broadcasted_iota(jnp.int32, (TOK, DH), 1)

    def fill_hot(t, carry):
        key_hot[rows_of(t), :] = jnp.where(lane == t, 1.0, 0.0).astype(jnp.bfloat16)
        return carry

    lax.fori_loop(0, CHIPS, fill_hot, 0)
    bias[...] = jnp.zeros_like(bias)
    tiles_copy.wait()
    bias[:, 0:CHIPS] = jnp.where(tile_buf[...] == 1, 0.0, MASKED)

    def all_of(ref, send_sem, recv_sem):
        return pltpu.make_async_remote_copy(
            src_ref=ref, dst_ref=ref, send_sem=send_sem, recv_sem=recv_sem,
            device_id={"branch": 1 - branch}, device_id_type=MESH)

    def first_rows(ref, count):
        return ref.at[pl.ds(0, count * TOK)]

    def send_q(n, carry):
        pz, px = to_partner(z, x, n)

        @pl.when(px < HEADS_IN_PLANE)
        def _():
            query_copy(n, pz, px).start()
        return carry

    lax.fori_loop(1, CHIPS, send_q, 0)

    def pair_copy(block):
        return pltpu.make_async_remote_copy(
            src_ref=own_o.at[block], dst_ref=partner_o.at[block],
            send_sem=pair_send.at[0], recv_sem=pair_recv.at[block],
            device_id={"branch": 1 - branch}, device_id_type=MESH)

    out_columns = pl.ds(pl.multiple_of(lax.rem(head, heads_of_half) * DH, DH), DH)

    def result_copy(n, block, part):
        pz, px = from_partner(z, x, n)
        return pltpu.make_async_remote_copy(
            src_ref=mixed.at[block, pl.ds(part * TOK, TOK)], dst_ref=out_ref.at[:, out_columns],
            send_sem=o_send.at[0], recv_sem=o_recv.at[0],
            device_id={"seq": pz * WIDTH + px}, device_id_type=MESH)

    def own_result_copy():
        return pltpu.make_async_copy(
            mixed.at[0, pl.ds(0, TOK)], out_ref.at[:, out_columns], local_sem.at[3])

    def combine(block):
        pair_copy(block).wait_recv()
        mine = own_o[block].astype(jnp.float32)
        other = partner_o[block].astype(jnp.float32)
        cond = jnp.where(branch == 0, mine, other)
        uncond = jnp.where(branch == 0, other, mine)
        mixed[block] = (uncond + GUIDE * (cond - uncond)).astype(jnp.bfloat16)
        for part in range(PAIR):
            n = block * PAIR + part

            @pl.when(n == 0)
            def _():
                own_result_copy().start()

            @pl.when(n != 0)
            def _():
                result_copy(n, block, part).start()

    def wait_queries(block):
        if isinstance(block, int) and block == 0:
            rows = pl.ds(TOK, TOK)
        else:
            rows = pl.ds(pl.multiple_of(block * BQ, BQ), BQ)
        all_of(q_buf.at[rows], q_send.at[0], q_recv.at[block]).wait_recv()

    def extended_query(block):
        parts = []
        for part in range(PAIR):
            n = block * PAIR + part
            pz, px = from_partner(z, x, n)
            row = bias[pl.ds(pz * WIDTH + px, 1), :]
            parts.append(jnp.concatenate(
                [q_buf[rows_of(n), :], jnp.broadcast_to(row, (TOK, DH)).astype(jnp.bfloat16)], axis=1))
        return jnp.concatenate(parts, axis=0)

    scale = math.log2(math.e) / math.sqrt(DH)

    def score(query, s_ref, chunk, top):
        keys = jnp.concatenate(
            [k_buf[chunk * KC:(chunk + 1) * KC, :], key_hot[chunk * KC:(chunk + 1) * KC, :]], axis=1)
        s = lax.dot_general(keys, query, (((1,), (1,)), ((), ())), preferred_element_type=jnp.float32)
        s_ref[chunk * KC:(chunk + 1) * KC, :] = s
        return jnp.maximum(top, jnp.max(s.reshape(KC // 8, 8, BQ), axis=0))

    def weigh(s_ref, top, chunk, total, row_total):
        s = s_ref[chunk * KC:(chunk + 1) * KC, :].reshape(KC // 8, 8, BQ)
        exponent = jnp.exp2(s * scale - top[None])
        weights = exponent.reshape(KC, BQ).astype(jnp.bfloat16)
        total = total + jnp.dot(
            v_t[:, chunk * KC:(chunk + 1) * KC], weights, preferred_element_type=jnp.float32)
        return total, row_total + jnp.sum(exponent, axis=0)

    lowest = jnp.full((8, BQ), -3e38, jnp.float32)

    def settle(top):
        return jnp.broadcast_to(jnp.max(top, axis=0, keepdims=True) * scale, (8, BQ))

    def finish(block, total, row_total):
        inverse = jnp.broadcast_to(1.0 / jnp.sum(row_total, axis=0, keepdims=True), (8, BQ))
        o = (total.reshape(DH // 8, 8, BQ) * inverse[None]).reshape(DH, BQ)
        own_o[block] = o.T.astype(jnp.bfloat16)

        @pl.when(jnp.logical_not(combines))
        def _():
            pair_copy(block).start()

    def half(block, following, top, s_now, s_next):
        if following is not None:
            wait_queries(following)
            query = extended_query(following)
        new_top = lowest
        total = jnp.zeros((DH, BQ), jnp.float32)
        row_total = jnp.zeros((8, BQ), jnp.float32)
        for chunk in range(CHUNKS):
            if following is not None:
                new_top = score(query, s_next, chunk, new_top)
            total, row_total = weigh(s_now, top, chunk, total, row_total)
        finish(block, total, row_total)

        @pl.when(jnp.logical_and(combines, block > 0))
        def _():
            combine(block - 1)
        return settle(new_top)

    @pl.when(owner)
    def _():
        for copy in own_copies():
            copy.wait()
        all_of(first_rows(k_buf, CHIPS - 1), kv_send.at[0], kv_recv.at[0]).wait_recv()
        all_of(first_rows(v_buf, CHIPS - 1), kv_send.at[1], kv_recv.at[1]).wait_recv()
        wait_queries(0)
        query = extended_query(0)
        top = lowest
        for chunk in range(CHUNKS):
            top = score(query, s_a, chunk, top)
            turned = slice(chunk * KC, (chunk + 1) * KC)
            v_t[:, turned] = v_buf[turned, :].T
        top = settle(top)

        def two_blocks(step, top):
            top = half(2 * step, 2 * step + 1, top, s_a, s_b)
            return half(2 * step + 1, 2 * step + 2, top, s_b, s_a)

        top = lax.fori_loop(0, BLOCKS // 2 - 1, two_blocks, top)
        top = half(BLOCKS - 2, BLOCKS - 1, top, s_a, s_b)
        half(BLOCKS - 1, None, top, s_b, s_a)

        @pl.when(combines)
        def _():
            combine(BLOCKS - 1)
            own_result_copy().wait()

            all_of(first_rows(q_buf, CHIPS - 1), o_send.at[0], o_recv.at[0]).wait_send()

        @pl.when(jnp.logical_not(combines))
        def _():
            all_of(own_o, pair_send.at[0], pair_recv.at[0]).wait_send()

    def wait_sent(count):
        all_of(first_rows(k_buf, count), kv_send.at[0], kv_recv.at[0]).wait_send()
        all_of(first_rows(v_buf, count), kv_send.at[1], kv_recv.at[1]).wait_send()
        all_of(first_rows(q_buf, count), q_send.at[0], q_recv.at[0]).wait_send()

    owners = PLANES * HEADS_IN_PLANE

    @pl.when(owner)
    def _():
        wait_sent(owners - 1)

    @pl.when(jnp.logical_not(owner))
    def _():
        wait_sent(owners)

    own_tile = jnp.logical_and(owner, combines)

    @pl.when(own_tile)
    def _():
        all_of(out_ref.at[:, pl.ds(0, (heads_of_half - 1) * DH)], o_send.at[0], o_recv.at[0]).wait_recv()

    @pl.when(jnp.logical_not(own_tile))
    def _():
        all_of(out_ref, o_send.at[0], o_recv.at[0]).wait_recv()


def shards(qkv, tiles):
    tok_rows, width = qkv.shape[1], qkv.shape[3]
    outgoing = qkv[0].transpose(1, 0, 2)
    bf16, f32 = jnp.bfloat16, jnp.float32
    dma = pltpu.SemaphoreType.DMA
    return pl.pallas_call(
        kernel,
        out_shape=pltpu.VMEM((tok_rows, width // 2), bf16),
        in_specs=[pl.BlockSpec(memory_space=pl.ANY), pl.BlockSpec(memory_space=pl.ANY)],
        out_specs=pl.BlockSpec(memory_space=pltpu.VMEM),
        scratch_shapes=[
            pltpu.VMEM((SEQ, DH), bf16),
            pltpu.VMEM((SEQ, DH), bf16),
            pltpu.VMEM((SEQ, DH), bf16),
            pltpu.VMEM((SEQ, DH), bf16),
            pltpu.VMEM((DH, SEQ), bf16),
            pltpu.VMEM((CHIPS, CHIPS), jnp.int32),
            pltpu.VMEM((CHIPS, DH), f32),
            pltpu.VMEM((SEQ, BQ), f32),
            pltpu.VMEM((SEQ, BQ), f32),
            pltpu.VMEM((BLOCKS, BQ, DH), bf16),
            pltpu.VMEM((BLOCKS, BQ, DH), bf16),
            pltpu.VMEM((BLOCKS, BQ, DH), bf16),
            dma((2,)), dma((2,)),
            dma((1,)), dma((BLOCKS,)),
            dma((1,)), dma((BLOCKS,)),
            dma((1,)), dma((1,)),
            dma((5,)),
        ],
        compiler_params=pltpu.CompilerParams(
            collective_id=0, has_side_effects=True, vmem_limit_bytes=60 * 2**20),
        cost_estimate=pl.CostEstimate(
            flops=4 * SEQ * SEQ * DH, bytes_accessed=4 * SEQ * DH * 2, transcendentals=SEQ * SEQ),
    )(outgoing, tiles)


def solution(mesh):
    in_specs = (P("branch", ("group", "seq"), None, None), P("group", None, None))
    out_specs = P(("group", "seq"), "branch")
    return jax.shard_map(shards, mesh=mesh, in_specs=in_specs, out_specs=out_specs, check_vma=False)
```

```python
import functools
import math

import jax
import jax.numpy as jnp
from jax import lax
from jax.experimental import pallas as pl
from jax.experimental.pallas import tpu as pltpu
from jax.sharding import PartitionSpec as P

MESH = pl.DeviceIdType.MESH
GUIDE = 5.0
MASKED = -1e30

PLANES, WIDTH = 8, 4
CHIPS = PLANES * WIDTH
HEADS_IN_PLANE = 3
TOK = 128
DH = 128
SEQ = CHIPS * TOK
PAIR = 2
BQ = PAIR * TOK
BLOCKS = CHIPS // PAIR
EARLY = 2 * PAIR
LAG = 2
KC = 1024
CHUNKS = SEQ // KC


def offset(n):
    turn = lax.rem(n, PLANES)
    distance = lax.rem(PLANES // 2 - turn // 2, PLANES // 2)
    backward = lax.rem(turn, 2)
    dx = lax.rem(n // PLANES + turn, WIDTH)
    dz = jnp.where(backward == 0, distance, jnp.where(distance == 0, 4, PLANES - distance))
    return dz, dx


def to_partner(z, x, n):
    dz, dx = offset(n)
    return lax.rem(z + dz, PLANES), lax.rem(x + dx, WIDTH)


def from_partner(z, x, n):
    dz, dx = offset(n)
    return lax.rem(z - dz + PLANES, PLANES), lax.rem(x - dx + WIDTH, WIDTH)


def owned_head(z, x):
    return z * HEADS_IN_PLANE + jnp.minimum(x, HEADS_IN_PLANE - 1)


def rows_of(index):
    return pl.ds(pl.multiple_of(index * TOK, TOK), TOK)


def kernel(
    send_ref, tiles_ref, out_ref,
    k_buf, v_buf, q_buf, key_hot, v_t, tile_buf, bias, s_a, s_b, own_o, partner_o, mixed,
    kv_send, kv_recv, q_send, q_recv, pair_send, pair_recv, o_send, o_recv, local_sem,
):
    seq = lax.axis_index("seq")
    branch = lax.axis_index("branch")
    z, x = seq // WIDTH, lax.rem(seq, WIDTH)
    owner = x < HEADS_IN_PLANE
    head = owned_head(z, x)
    heads_of_half = out_ref.shape[1] // DH
    my_half = head // heads_of_half
    combines = my_half == branch

    tiles_copy = pltpu.make_async_copy(tiles_ref.at[head], tile_buf, local_sem.at[4])
    tiles_copy.start()
    barrier = pltpu.get_barrier_semaphore()

    def greet(n, carry):
        pz, px = to_partner(z, x, n)
        pl.semaphore_signal(barrier, inc=1, device_id={"seq": pz * WIDTH + px}, device_id_type=MESH)
        return carry

    lax.fori_loop(1, CHIPS, greet, 0)
    pl.semaphore_signal(barrier, inc=1, device_id={"branch": 1 - branch}, device_id_type=MESH)
    pl.semaphore_wait(barrier, CHIPS)

    def block_of(which, part):
        return send_ref.at[part, :, pl.ds(pl.multiple_of(which * DH, DH), DH)]

    def key_copy(n, pz, px):
        chosen = owned_head(pz, px)
        return pltpu.make_async_remote_copy(
            src_ref=block_of(chosen, 1), dst_ref=k_buf.at[rows_of(seq)],
            send_sem=kv_send.at[0], recv_sem=kv_recv.at[0],
            device_id={"seq": pz * WIDTH + px}, device_id_type=MESH)

    def value_copy(n, pz, px):
        chosen = owned_head(pz, px)
        return pltpu.make_async_remote_copy(
            src_ref=block_of(chosen, 2), dst_ref=v_buf.at[rows_of(seq)],
            send_sem=kv_send.at[1], recv_sem=kv_recv.at[1],
            device_id={"seq": pz * WIDTH + px}, device_id_type=MESH)

    def query_copy(n, pz, px):
        chosen = owned_head(pz, px)
        return pltpu.make_async_remote_copy(
            src_ref=block_of(chosen, 0), dst_ref=q_buf.at[rows_of(n)],
            send_sem=q_send.at[0], recv_sem=q_recv.at[n // PAIR],
            device_id={"seq": pz * WIDTH + px}, device_id_type=MESH)

    def own_copies():
        return (
            pltpu.make_async_copy(block_of(head, 1), k_buf.at[rows_of(seq)], local_sem.at[0]),
            pltpu.make_async_copy(block_of(head, 2), v_buf.at[rows_of(seq)], local_sem.at[1]),
            pltpu.make_async_copy(block_of(head, 0), q_buf.at[rows_of(0)], local_sem.at[2]),
        )

    def sends(copy):
        def send(n, carry):
            pz, px = to_partner(z, x, n)

            @pl.when(px < HEADS_IN_PLANE)
            def _():
                copy(n, pz, px).start()
            return carry
        return send

    lax.fori_loop(1, CHIPS, sends(key_copy), 0)
    lax.fori_loop(1, EARLY, sends(query_copy), 0)
    lax.fori_loop(1, CHIPS, sends(value_copy), 0)
    lax.fori_loop(EARLY, CHIPS, sends(query_copy), 0)

    @pl.when(owner)
    def _():
        for copy in own_copies():
            copy.start()

    lane = lax.broadcasted_iota(jnp.int32, (TOK, DH), 1)

    def fill_hot(t, carry):
        key_hot[rows_of(t), :] = jnp.where(lane == t, 1.0, 0.0).astype(jnp.bfloat16)
        return carry

    lax.fori_loop(0, CHIPS, fill_hot, 0)
    bias[...] = jnp.zeros_like(bias)
    tiles_copy.wait()
    bias[:, 0:CHIPS] = jnp.where(tile_buf[...] == 1, 0.0, MASKED)

    def all_of(ref, send_sem, recv_sem):
        return pltpu.make_async_remote_copy(
            src_ref=ref, dst_ref=ref, send_sem=send_sem, recv_sem=recv_sem,
            device_id={"branch": 1 - branch}, device_id_type=MESH)

    def first_rows(ref, count):
        return ref.at[pl.ds(0, count * TOK)]

    def pair_copy(block):
        return pltpu.make_async_remote_copy(
            src_ref=own_o.at[block], dst_ref=partner_o.at[block],
            send_sem=pair_send.at[0], recv_sem=pair_recv.at[block],
            device_id={"branch": 1 - branch}, device_id_type=MESH)

    out_columns = pl.ds(pl.multiple_of(lax.rem(head, heads_of_half) * DH, DH), DH)

    def result_copy(n, block, part):
        pz, px = from_partner(z, x, n)
        return pltpu.make_async_remote_copy(
            src_ref=mixed.at[block, pl.ds(part * TOK, TOK)], dst_ref=out_ref.at[:, out_columns],
            send_sem=o_send.at[0], recv_sem=o_recv.at[0],
            device_id={"seq": pz * WIDTH + px}, device_id_type=MESH)

    def own_result_copy():
        return pltpu.make_async_copy(
            mixed.at[0, pl.ds(0, TOK)], out_ref.at[:, out_columns], local_sem.at[3])

    def mix(block):
        mine = own_o[block].astype(jnp.float32)
        other = partner_o[block].astype(jnp.float32)
        cond = jnp.where(branch == 0, mine, other)
        uncond = jnp.where(branch == 0, other, mine)
        mixed[block] = (uncond + GUIDE * (cond - uncond)).astype(jnp.bfloat16)

    def send_results(block):
        for part in range(PAIR):
            n = block * PAIR + part

            @pl.when(n == 0)
            def _():
                own_result_copy().start()

            @pl.when(n != 0)
            def _():
                result_copy(n, block, part).start()

    def wait_queries(block):
        if isinstance(block, int) and block == 0:
            rows = pl.ds(TOK, TOK)
        else:
            rows = pl.ds(pl.multiple_of(block * BQ, BQ), BQ)
        all_of(q_buf.at[rows], q_send.at[0], q_recv.at[block]).wait_recv()

    def extended_query(block):
        parts = []
        for part in range(PAIR):
            n = block * PAIR + part
            pz, px = from_partner(z, x, n)
            row = bias[pl.ds(pz * WIDTH + px, 1), :]
            parts.append(jnp.concatenate(
                [q_buf[rows_of(n), :], jnp.broadcast_to(row, (TOK, DH)).astype(jnp.bfloat16)], axis=1))
        return jnp.concatenate(parts, axis=0)

    scale = math.log2(math.e) / math.sqrt(DH)

    def score(query, s_ref, chunk, top):
        keys = jnp.concatenate(
            [k_buf[chunk * KC:(chunk + 1) * KC, :], key_hot[chunk * KC:(chunk + 1) * KC, :]], axis=1)
        s = lax.dot_general(keys, query, (((1,), (1,)), ((), ())), preferred_element_type=jnp.float32)
        s_ref[chunk * KC:(chunk + 1) * KC, :] = s
        return jnp.maximum(top, jnp.max(s.reshape(KC // 8, 8, BQ), axis=0))

    def weigh(s_ref, top, chunk, total, row_total):
        s = s_ref[chunk * KC:(chunk + 1) * KC, :].reshape(KC // 8, 8, BQ)
        exponent = jnp.exp2(s * scale - top[None])
        weights = exponent.reshape(KC, BQ).astype(jnp.bfloat16)
        total = total + jnp.dot(
            v_t[:, chunk * KC:(chunk + 1) * KC], weights, preferred_element_type=jnp.float32)
        return total, row_total + jnp.sum(exponent, axis=0)

    lowest = jnp.full((8, BQ), -3e38, jnp.float32)

    def settle(top):
        return jnp.broadcast_to(jnp.max(top, axis=0, keepdims=True) * scale, (8, BQ))

    def finish(block, total, row_total):
        inverse = jnp.broadcast_to(1.0 / jnp.sum(row_total, axis=0, keepdims=True), (8, BQ))
        o = (total.reshape(DH // 8, 8, BQ) * inverse[None]).reshape(DH, BQ)
        own_o[block] = o.T.astype(jnp.bfloat16)

        @pl.when(jnp.logical_not(combines))
        def _():
            pair_copy(block).start()

    def half(block, following, top, s_now, s_next, first=False, mixing=True):
        if following is not None:
            wait_queries(following)
            query = extended_query(following)
        if mixing:
            @pl.when(combines)
            def _():
                pair_copy(block - LAG).wait_recv()

            mix(block - LAG)
        new_top = lowest
        total = jnp.zeros((DH, BQ), jnp.float32)
        row_total = jnp.zeros((8, BQ), jnp.float32)
        for chunk in range(CHUNKS):
            if following is not None:
                new_top = score(query, s_next, chunk, new_top)
            if first:
                turned = slice(chunk * KC, (chunk + 1) * KC)
                v_t[:, turned] = v_buf[turned, :].T
            total, row_total = weigh(s_now, top, chunk, total, row_total)
        finish(block, total, row_total)
        if mixing:
            @pl.when(combines)
            def _():
                send_results(block - LAG)
        return settle(new_top)

    @pl.when(owner)
    def _():
        for copy in own_copies():
            copy.wait()
        all_of(first_rows(k_buf, CHIPS - 1), kv_send.at[0], kv_recv.at[0]).wait_recv()
        wait_queries(0)
        query = extended_query(0)
        top = lowest
        for chunk in range(CHUNKS):
            top = score(query, s_a, chunk, top)
        top = settle(top)
        all_of(first_rows(v_buf, CHIPS - 1), kv_send.at[1], kv_recv.at[1]).wait_recv()
        top = half(0, 1, top, s_a, s_b, first=True, mixing=False)
        top = half(1, 2, top, s_b, s_a, mixing=False)

        def two_blocks(step, top):
            top = half(2 * step, 2 * step + 1, top, s_a, s_b)
            return half(2 * step + 1, 2 * step + 2, top, s_b, s_a)

        top = lax.fori_loop(1, BLOCKS // 2 - 1, two_blocks, top)
        top = half(BLOCKS - 2, BLOCKS - 1, top, s_a, s_b)

        @pl.when(combines)
        def _():
            pair_copy(BLOCKS - 3).wait_recv()
            mix(BLOCKS - 3)
            send_results(BLOCKS - 3)

        half(BLOCKS - 1, None, top, s_b, s_a, mixing=False)

        @pl.when(combines)
        def _():
            for block in range(BLOCKS - LAG, BLOCKS):
                pair_copy(block).wait_recv()
                mix(block)
                send_results(block)
            own_result_copy().wait()

            all_of(first_rows(q_buf, CHIPS - 1), o_send.at[0], o_recv.at[0]).wait_send()

        @pl.when(jnp.logical_not(combines))
        def _():
            all_of(own_o, pair_send.at[0], pair_recv.at[0]).wait_send()

    def wait_sent(count):
        all_of(first_rows(k_buf, count), kv_send.at[0], kv_recv.at[0]).wait_send()
        all_of(first_rows(v_buf, count), kv_send.at[1], kv_recv.at[1]).wait_send()
        all_of(first_rows(q_buf, count), q_send.at[0], q_recv.at[0]).wait_send()

    owners = PLANES * HEADS_IN_PLANE

    @pl.when(owner)
    def _():
        wait_sent(owners - 1)

    @pl.when(jnp.logical_not(owner))
    def _():
        wait_sent(owners)

    own_tile = jnp.logical_and(owner, combines)

    @pl.when(own_tile)
    def _():
        all_of(out_ref.at[:, pl.ds(0, (heads_of_half - 1) * DH)], o_send.at[0], o_recv.at[0]).wait_recv()

    @pl.when(jnp.logical_not(own_tile))
    def _():
        all_of(out_ref, o_send.at[0], o_recv.at[0]).wait_recv()


def shards(qkv, tiles):
    tok_rows, width = qkv.shape[1], qkv.shape[3]
    outgoing = qkv[0].transpose(1, 0, 2)
    bf16, f32 = jnp.bfloat16, jnp.float32
    dma = pltpu.SemaphoreType.DMA
    return pl.pallas_call(
        kernel,
        out_shape=pltpu.VMEM((tok_rows, width // 2), bf16),
        in_specs=[pl.BlockSpec(memory_space=pl.ANY), pl.BlockSpec(memory_space=pl.ANY)],
        out_specs=pl.BlockSpec(memory_space=pltpu.VMEM),
        scratch_shapes=[
            pltpu.VMEM((SEQ, DH), bf16),
            pltpu.VMEM((SEQ, DH), bf16),
            pltpu.VMEM((SEQ, DH), bf16),
            pltpu.VMEM((SEQ, DH), bf16),
            pltpu.VMEM((DH, SEQ), bf16),
            pltpu.VMEM((CHIPS, CHIPS), jnp.int32),
            pltpu.VMEM((CHIPS, DH), f32),
            pltpu.VMEM((SEQ, BQ), f32),
            pltpu.VMEM((SEQ, BQ), f32),
            pltpu.VMEM((BLOCKS, BQ, DH), bf16),
            pltpu.VMEM((BLOCKS, BQ, DH), bf16),
            pltpu.VMEM((BLOCKS, BQ, DH), bf16),
            dma((2,)), dma((2,)),
            dma((1,)), dma((BLOCKS,)),
            dma((1,)), dma((BLOCKS,)),
            dma((1,)), dma((1,)),
            dma((5,)),
        ],
        compiler_params=pltpu.CompilerParams(
            collective_id=0, has_side_effects=True, vmem_limit_bytes=60 * 2**20),
        cost_estimate=pl.CostEstimate(
            flops=4 * SEQ * SEQ * DH, bytes_accessed=4 * SEQ * DH * 2, transcendentals=SEQ * SEQ),
    )(outgoing, tiles)


def solution(mesh):
    in_specs = (P("branch", ("group", "seq"), None, None), P("group", None, None))
    out_specs = P(("group", "seq"), "branch")
    return jax.shard_map(shards, mesh=mesh, in_specs=in_specs, out_specs=out_specs, check_vma=False)
```

```python
import functools
import math

import jax
import jax.numpy as jnp
from jax import lax
from jax.experimental import pallas as pl
from jax.experimental.pallas import tpu as pltpu
from jax.sharding import PartitionSpec as P

MESH = pl.DeviceIdType.MESH
GUIDE = 5.0
MASKED = -1e30

PLANES, WIDTH = 8, 4
CHIPS = PLANES * WIDTH
HEADS_IN_PLANE = 3
TOK = 128
DH = 128
SEQ = CHIPS * TOK
PAIR = 2
BQ = PAIR * TOK
BLOCKS = CHIPS // PAIR
EARLY = 3 * PAIR
VG = 24
LAG = 2
KC = 512
CHUNKS = SEQ // KC


def offset(n):
    turn = lax.rem(n, PLANES)
    distance = lax.rem(PLANES // 2 - turn // 2, PLANES // 2)
    backward = lax.rem(turn, 2)
    dx = lax.rem(n // PLANES + turn, WIDTH)
    dz = jnp.where(backward == 0, distance, jnp.where(distance == 0, 4, PLANES - distance))
    return dz, dx


def to_partner(z, x, n):
    dz, dx = offset(n)
    return lax.rem(z + dz, PLANES), lax.rem(x + dx, WIDTH)


def from_partner(z, x, n):
    dz, dx = offset(n)
    return lax.rem(z - dz + PLANES, PLANES), lax.rem(x - dx + WIDTH, WIDTH)


def owned_head(z, x):
    return z * HEADS_IN_PLANE + jnp.minimum(x, HEADS_IN_PLANE - 1)


def rows_of(index):
    return pl.ds(pl.multiple_of(index * TOK, TOK), TOK)


def kernel(
    send_ref, tiles_ref, out_ref,
    k_buf, v_buf, q_buf, key_hot, v_t, tile_buf, bias, s_a, s_b, own_o, partner_o, mixed,
    kv_send, kv_recv, q_send, q_recv, pair_send, pair_recv, o_send, o_recv, local_sem,
):
    seq = lax.axis_index("seq")
    branch = lax.axis_index("branch")
    z, x = seq // WIDTH, lax.rem(seq, WIDTH)
    owner = x < HEADS_IN_PLANE
    head = owned_head(z, x)
    heads_of_half = out_ref.shape[1] // DH
    my_half = head // heads_of_half
    combines = my_half == branch

    tiles_copy = pltpu.make_async_copy(tiles_ref.at[head], tile_buf, local_sem.at[4])
    tiles_copy.start()
    barrier = pltpu.get_barrier_semaphore()

    def greet(n, carry):
        pz, px = to_partner(z, x, n)
        pl.semaphore_signal(barrier, inc=1, device_id={"seq": pz * WIDTH + px}, device_id_type=MESH)
        return carry

    lax.fori_loop(1, CHIPS, greet, 0)
    pl.semaphore_signal(barrier, inc=1, device_id={"branch": 1 - branch}, device_id_type=MESH)
    pl.semaphore_wait(barrier, CHIPS)

    def block_of(which, part):
        return send_ref.at[part, :, pl.ds(pl.multiple_of(which * DH, DH), DH)]

    def key_copy(n, pz, px):
        chosen = owned_head(pz, px)
        return pltpu.make_async_remote_copy(
            src_ref=block_of(chosen, 1), dst_ref=k_buf.at[rows_of(seq)],
            send_sem=kv_send.at[0], recv_sem=kv_recv.at[0],
            device_id={"seq": pz * WIDTH + px}, device_id_type=MESH)

    def value_copy(n, pz, px):
        chosen = owned_head(pz, px)
        return pltpu.make_async_remote_copy(
            src_ref=block_of(chosen, 2), dst_ref=v_buf.at[rows_of(seq)],
            send_sem=kv_send.at[1 + n // VG], recv_sem=kv_recv.at[1],
            device_id={"seq": pz * WIDTH + px}, device_id_type=MESH)

    def query_copy(n, pz, px):
        chosen = owned_head(pz, px)
        return pltpu.make_async_remote_copy(
            src_ref=block_of(chosen, 0), dst_ref=q_buf.at[rows_of(n)],
            send_sem=q_send.at[0], recv_sem=q_recv.at[n // PAIR],
            device_id={"seq": pz * WIDTH + px}, device_id_type=MESH)

    def own_copies():
        return (
            pltpu.make_async_copy(block_of(head, 1), k_buf.at[rows_of(seq)], local_sem.at[0]),
            pltpu.make_async_copy(block_of(head, 2), v_buf.at[rows_of(seq)], local_sem.at[1]),
            pltpu.make_async_copy(block_of(head, 0), q_buf.at[rows_of(0)], local_sem.at[2]),
        )

    def sends(copy):
        def send(n, carry):
            pz, px = to_partner(z, x, n)

            @pl.when(px < HEADS_IN_PLANE)
            def _():
                copy(n, pz, px).start()
            return carry
        return send

    lax.fori_loop(1, CHIPS, sends(key_copy), 0)
    lax.fori_loop(1, EARLY, sends(query_copy), 0)
    lax.fori_loop(1, CHIPS, sends(value_copy), 0)
    def rest_of_q():
        lax.fori_loop(EARLY, CHIPS, sends(query_copy), 0)

    def v_sent(group, mine):
        lo, hi = (0, VG) if group == 0 else (VG, CHIPS)
        count = (hi - lo) // PLANES * (PLANES * HEADS_IN_PLANE // WIDTH) - (mine if group == 0 else 0)
        all_of(first_rows(v_buf, count), kv_send.at[1 + group], kv_recv.at[1]).wait_send()

    @pl.when(owner)
    def _():
        for copy in own_copies():
            copy.start()

    lane = lax.broadcasted_iota(jnp.int32, (TOK, DH), 1)

    def fill_hot(t, carry):
        key_hot[rows_of(t), :] = jnp.where(lane == t, 1.0, 0.0).astype(jnp.bfloat16)
        return carry

    lax.fori_loop(0, CHIPS, fill_hot, 0)
    bias[...] = jnp.zeros_like(bias)
    tiles_copy.wait()
    bias[:, 0:CHIPS] = jnp.where(tile_buf[...] == 1, 0.0, MASKED)

    def all_of(ref, send_sem, recv_sem):
        return pltpu.make_async_remote_copy(
            src_ref=ref, dst_ref=ref, send_sem=send_sem, recv_sem=recv_sem,
            device_id={"branch": 1 - branch}, device_id_type=MESH)

    def first_rows(ref, count):
        return ref.at[pl.ds(0, count * TOK)]

    def pair_copy(block):
        return pltpu.make_async_remote_copy(
            src_ref=own_o.at[block], dst_ref=partner_o.at[block],
            send_sem=pair_send.at[0], recv_sem=pair_recv.at[block],
            device_id={"branch": 1 - branch}, device_id_type=MESH)

    out_columns = pl.ds(pl.multiple_of(lax.rem(head, heads_of_half) * DH, DH), DH)

    def result_copy(n, block, part):
        pz, px = from_partner(z, x, n)
        return pltpu.make_async_remote_copy(
            src_ref=mixed.at[block, pl.ds(part * TOK, TOK)], dst_ref=out_ref.at[:, out_columns],
            send_sem=o_send.at[0], recv_sem=o_recv.at[0],
            device_id={"seq": pz * WIDTH + px}, device_id_type=MESH)

    def own_result_copy():
        return pltpu.make_async_copy(
            mixed.at[0, pl.ds(0, TOK)], out_ref.at[:, out_columns], local_sem.at[3])

    def mix(block):
        mine = own_o[block].astype(jnp.float32)
        other = partner_o[block].astype(jnp.float32)
        cond = jnp.where(branch == 0, mine, other)
        uncond = jnp.where(branch == 0, other, mine)
        mixed[block] = (uncond + GUIDE * (cond - uncond)).astype(jnp.bfloat16)

    def send_results(block):
        for part in range(PAIR):
            n = block * PAIR + part

            @pl.when(n == 0)
            def _():
                own_result_copy().start()

            @pl.when(n != 0)
            def _():
                result_copy(n, block, part).start()

    def wait_queries(block):
        if isinstance(block, int) and block == 0:
            rows = pl.ds(TOK, TOK)
        else:
            rows = pl.ds(pl.multiple_of(block * BQ, BQ), BQ)
        all_of(q_buf.at[rows], q_send.at[0], q_recv.at[block]).wait_recv()

    def extended_query(block):
        parts = []
        for part in range(PAIR):
            n = block * PAIR + part
            pz, px = from_partner(z, x, n)
            row = bias[pl.ds(pz * WIDTH + px, 1), :]
            parts.append(jnp.concatenate(
                [q_buf[rows_of(n), :], jnp.broadcast_to(row, (TOK, DH)).astype(jnp.bfloat16)], axis=1))
        return jnp.concatenate(parts, axis=0)

    scale = math.log2(math.e) / math.sqrt(DH)

    def score(query, s_ref, chunk, top):
        keys = jnp.concatenate(
            [k_buf[chunk * KC:(chunk + 1) * KC, :], key_hot[chunk * KC:(chunk + 1) * KC, :]], axis=1)
        s = lax.dot_general(keys, query, (((1,), (1,)), ((), ())), preferred_element_type=jnp.float32)
        s_ref[chunk * KC:(chunk + 1) * KC, :] = s
        return jnp.maximum(top, jnp.max(s.reshape(KC // 8, 8, BQ), axis=0))

    def weigh(s_ref, top, chunk, total, row_total):
        s = s_ref[chunk * KC:(chunk + 1) * KC, :].reshape(KC // 8, 8, BQ)
        exponent = jnp.exp2(s * scale - top[None])
        weights = exponent.reshape(KC, BQ).astype(jnp.bfloat16)
        total = total + jnp.dot(
            v_t[:, chunk * KC:(chunk + 1) * KC], weights, preferred_element_type=jnp.float32)
        return total, row_total + jnp.sum(exponent, axis=0)

    lowest = jnp.full((8, BQ), -3e38, jnp.float32)

    def settle(top):
        return jnp.broadcast_to(jnp.max(top, axis=0, keepdims=True) * scale, (8, BQ))

    def finish(block, total, row_total):
        inverse = jnp.broadcast_to(1.0 / jnp.sum(row_total, axis=0, keepdims=True), (8, BQ))
        o = (total.reshape(DH // 8, 8, BQ) * inverse[None]).reshape(DH, BQ)
        own_o[block] = o.T.astype(jnp.bfloat16)

        @pl.when(jnp.logical_not(combines))
        def _():
            pair_copy(block).start()

    def half(block, following, top, s_now, s_next, first=False, mixing=True):
        if following is not None:
            wait_queries(following)
            query = extended_query(following)
        if mixing:
            @pl.when(combines)
            def _():
                pair_copy(block - LAG).wait_recv()

            mix(block - LAG)
        new_top = lowest
        total = jnp.zeros((DH, BQ), jnp.float32)
        row_total = jnp.zeros((8, BQ), jnp.float32)
        for chunk in range(CHUNKS):
            if following is not None:
                new_top = score(query, s_next, chunk, new_top)
            if first:
                turned = slice(chunk * KC, (chunk + 1) * KC)
                v_t[:, turned] = v_buf[turned, :].T
            total, row_total = weigh(s_now, top, chunk, total, row_total)
        finish(block, total, row_total)
        if mixing:
            @pl.when(combines)
            def _():
                send_results(block - LAG)
        return settle(new_top)

    @pl.when(owner)
    def _():
        for copy in own_copies():
            copy.wait()
        all_of(first_rows(k_buf, CHIPS - 1), kv_send.at[0], kv_recv.at[0]).wait_recv()
        wait_queries(0)
        query = extended_query(0)
        top = lowest
        for chunk in range(CHUNKS):
            top = score(query, s_a, chunk, top)
        top = settle(top)
        v_sent(0, 1)
        rest_of_q()
        all_of(first_rows(v_buf, CHIPS - 1), kv_send.at[1], kv_recv.at[1]).wait_recv()
        top = half(0, 1, top, s_a, s_b, first=True, mixing=False)
        top = half(1, 2, top, s_b, s_a, mixing=False)

        def two_blocks(step, top):
            top = half(2 * step, 2 * step + 1, top, s_a, s_b)
            return half(2 * step + 1, 2 * step + 2, top, s_b, s_a)

        top = lax.fori_loop(1, BLOCKS // 2 - 1, two_blocks, top)
        top = half(BLOCKS - 2, BLOCKS - 1, top, s_a, s_b)

        @pl.when(combines)
        def _():
            pair_copy(BLOCKS - 3).wait_recv()
            mix(BLOCKS - 3)
            send_results(BLOCKS - 3)

        half(BLOCKS - 1, None, top, s_b, s_a, mixing=False)

        @pl.when(combines)
        def _():
            for block in range(BLOCKS - LAG, BLOCKS):
                pair_copy(block).wait_recv()
                mix(block)
                send_results(block)
            own_result_copy().wait()

            all_of(first_rows(q_buf, CHIPS - 1), o_send.at[0], o_recv.at[0]).wait_send()

        @pl.when(jnp.logical_not(combines))
        def _():
            all_of(own_o, pair_send.at[0], pair_recv.at[0]).wait_send()

    def wait_sent(count):
        all_of(first_rows(k_buf, count), kv_send.at[0], kv_recv.at[0]).wait_send()
        v_sent(1, 0)
        all_of(first_rows(q_buf, count), q_send.at[0], q_recv.at[0]).wait_send()

    owners = PLANES * HEADS_IN_PLANE

    @pl.when(owner)
    def _():
        wait_sent(owners - 1)

    @pl.when(jnp.logical_not(owner))
    def _():
        v_sent(0, 0)
        rest_of_q()
        wait_sent(owners)

    own_tile = jnp.logical_and(owner, combines)

    @pl.when(own_tile)
    def _():
        all_of(out_ref.at[:, pl.ds(0, (heads_of_half - 1) * DH)], o_send.at[0], o_recv.at[0]).wait_recv()

    @pl.when(jnp.logical_not(own_tile))
    def _():
        all_of(out_ref, o_send.at[0], o_recv.at[0]).wait_recv()


def shards(qkv, tiles):
    tok_rows, width = qkv.shape[1], qkv.shape[3]
    outgoing = qkv[0].transpose(1, 0, 2)
    bf16, f32 = jnp.bfloat16, jnp.float32
    dma = pltpu.SemaphoreType.DMA
    return pl.pallas_call(
        kernel,
        out_shape=pltpu.VMEM((tok_rows, width // 2), bf16),
        in_specs=[pl.BlockSpec(memory_space=pl.ANY), pl.BlockSpec(memory_space=pl.ANY)],
        out_specs=pl.BlockSpec(memory_space=pltpu.VMEM),
        scratch_shapes=[
            pltpu.VMEM((SEQ, DH), bf16),
            pltpu.VMEM((SEQ, DH), bf16),
            pltpu.VMEM((SEQ, DH), bf16),
            pltpu.VMEM((SEQ, DH), bf16),
            pltpu.VMEM((DH, SEQ), bf16),
            pltpu.VMEM((CHIPS, CHIPS), jnp.int32),
            pltpu.VMEM((CHIPS, DH), f32),
            pltpu.VMEM((SEQ, BQ), f32),
            pltpu.VMEM((SEQ, BQ), f32),
            pltpu.VMEM((BLOCKS, BQ, DH), bf16),
            pltpu.VMEM((BLOCKS, BQ, DH), bf16),
            pltpu.VMEM((BLOCKS, BQ, DH), bf16),
            dma((3,)), dma((2,)),
            dma((1,)), dma((BLOCKS,)),
            dma((1,)), dma((BLOCKS,)),
            dma((1,)), dma((1,)),
            dma((5,)),
        ],
        compiler_params=pltpu.CompilerParams(
            collective_id=0, has_side_effects=True, vmem_limit_bytes=60 * 2**20),
        cost_estimate=pl.CostEstimate(
            flops=4 * SEQ * SEQ * DH, bytes_accessed=4 * SEQ * DH * 2, transcendentals=SEQ * SEQ),
    )(outgoing, tiles)


def solution(mesh):
    in_specs = (P("branch", ("group", "seq"), None, None), P("group", None, None))
    out_specs = P(("group", "seq"), "branch")
    return jax.shard_map(shards, mesh=mesh, in_specs=in_specs, out_specs=out_specs, check_vma=False)
```
